128 devices in a mesh: outer: 8 (over x, core), inner: 16 (over z, y).
Axes of the slice: x: 4, y: 4, z: 4, core: 2. Of those that a mesh axis runs over, the one named last changes fastest.
Arguments:
- query_vec: bfloat16 [131072, 256], P(('outer', 'inner')), may hold values from -40 to 40
- key_vec: bfloat16 [131072, 256], P(('outer', 'inner')), may hold values from -9 to 9
- value_vec: bfloat16 [131072, 256], P(('outer', 'inner')), may hold values from -6 to 6
- grad_out: bfloat16 [131072, 256], P(('outer', 'inner')), may hold values from -6 to 6
- chosen: int32 [128, 3], replicated, may hold values from 0 to 127, as said below
- layout: int32 [16], replicated, may hold values from 0 to 15, each once
Outputs:
- grad_query: bfloat16 [131072, 256], P(('outer', 'inner'))
- grad_key: bfloat16 [131072, 256], P(('outer', 'inner'))
- grad_value: bfloat16 [131072, 256], P(('outer', 'inner'))
The draws below stay inside these ranges and needn't reach their ends.
Inputs may be any that keep to these rules, and one draw needn't show every extreme that they name: `chosen`: row b lists the blocks picked by query block b's gate among all earlier blocks of the sequence: min(3, b) distinct blocks below b, and b itself in the remaining slots.
All inputs are finite; a program needn't handle non-finite values.
Results may differ from the reference program's by a relative error of at most 0.02.
Values may be sent and summed in bfloat16 or wider, within the bound.
A program may use at most 128 MiB of HBM per device.

```python
import math
import jax
import jax.numpy as jnp
from jax import lax

HEADS = 2
HD = 128
TOPK = 3
NB = 128
SEQ = 131072
N_INNER = 16


def draw_query_vec(key, part):
    key = jax.random.fold_in(key, 3)
    drawn = jax.random.truncated_normal(key, -4.0, 4.0, (SEQ, HEADS * HD)) * 2.0
    return drawn.astype(jnp.bfloat16)


def draw_key_vec(key, part):
    key = jax.random.fold_in(key, 5)
    drawn = jax.random.truncated_normal(key, -4.0, 4.0, (SEQ, HEADS * HD))
    return drawn.astype(jnp.bfloat16)


def draw_chosen(key, part):
    key = jax.random.fold_in(key, 11)
    block_ids = jnp.arange(NB, dtype=jnp.int32)
    positions = jnp.arange(NB, dtype=jnp.int32)[None, :]
    candidate_ok = positions < block_ids[:, None]
    ranking = jax.random.randint(key, (NB, NB), 0, 2 ** 20) * NB + positions
    ranking = jnp.where(candidate_ok, ranking, -1 - positions)
    top_values, top_slots = lax.top_k(ranking, TOPK)
    found = top_slots < block_ids[:, None]
    return jnp.where(found, top_slots, block_ids[:, None]).astype(jnp.int32)


def levels(rng, extent, pieces, smallest, largest):
    def one(dim, blocks):
        draws = jax.random.uniform(jax.random.fold_in(jax.random.fold_in(rng, 6), dim), (blocks,), jnp.float32, smallest / len(pieces), largest / len(pieces))
        return jnp.repeat(jnp.exp(draws), extent[dim] // blocks).reshape((-1,) + (1,) * (len(extent) - dim - 1))

    loudness = one(*pieces[0])
    for cut in pieces[1:]:
        loudness = loudness * one(*cut)
    return loudness


def centred(key, extent, spread, bound, split=(), kind=jnp.bfloat16):
    drawn = spread * jax.random.normal(key, extent, jnp.float32)
    if split:
        drawn = drawn * levels(key, extent, split, -0.22, 0.18)
    return jnp.clip(drawn, -bound, bound).astype(kind)


def setup_inputs(seed: int = 0) -> dict:
    key_of = jax.random.split(jax.random.key(seed), 7)
    return {
        "query_vec": draw_query_vec(jax.random.fold_in(key_of[6], 71), 0),
        "key_vec": draw_key_vec(jax.random.fold_in(key_of[6], 71), 0),
        "value_vec": centred(key_of[2], (SEQ, HEADS * HD), 1.0, 6.0, ((0, 128),)),
        "grad_out": centred(key_of[3], (SEQ, HEADS * HD), 1.0, 6.0, ((0, 128),)),
        "chosen": draw_chosen(jax.random.fold_in(key_of[6], 71), 0),
        "layout": jax.random.permutation(key_of[5], N_INNER).astype(jnp.int32),
    }


def reference(query_vec, key_vec, value_vec, grad_out, chosen, layout):
    blocks = chosen.shape[0]
    length = query_vec.shape[0] // blocks
    head_size = query_vec.shape[1] // HEADS
    score_scale = 1.0 / math.sqrt(head_size)
    positions = jnp.arange(N_INNER, dtype=jnp.int32)
    inverse = lax.optimization_barrier(jnp.sum(jnp.where(layout[:, None] == positions[None, :], positions[:, None], 0), axis=0)).astype(jnp.int32)

    def row_of(context):
        return (context // N_INNER * N_INNER + inverse[context % N_INNER]).astype(jnp.int32)
    query_blocks = query_vec.reshape(blocks, length, HEADS, head_size)
    key_blocks = key_vec.reshape(blocks, length, HEADS, head_size)
    value_blocks = value_vec.reshape(blocks, length, HEADS, head_size)
    grad_blocks = grad_out.reshape(blocks, length, HEADS, head_size)
    causal = jnp.arange(length)[None, :] <= jnp.arange(length)[:, None]
    tile_ids = jnp.arange(TOPK + 1)

    def visit_block(carried, block_id):
        sum_keys, sum_values = carried
        own_row = row_of(block_id)
        picked = chosen[block_id]
        row_list = jnp.concatenate([own_row[None], row_of(picked)]).astype(jnp.int32)
        is_valid = jnp.concatenate([jnp.array([True]), picked < block_id])
        queries = query_blocks[own_row].astype(jnp.float32)
        grads = grad_blocks[own_row].astype(jnp.float32)
        tile_keys = key_blocks[row_list].astype(jnp.float32)
        tile_values = value_blocks[row_list].astype(jnp.float32)
        scores = jnp.einsum('qhd,tkhd->thqk', queries, tile_keys) * score_scale
        allowed = jnp.where(tile_ids[:, None, None] == 0, causal[None], is_valid[:, None, None])
        scores = jnp.where(allowed[:, None], scores, -jnp.inf)
        row_max = lax.optimization_barrier(jnp.max(scores, axis=(0, 3)))
        totals_row = lax.optimization_barrier(jnp.sum(jnp.exp(scores - row_max[None, :, :, None]), axis=(0, 3)))
        log_total = row_max + jnp.log(totals_row)
        probabilities = jnp.exp(scores - log_total[None, :, :, None])
        weights = lax.optimization_barrier(probabilities.astype(jnp.bfloat16)).astype(jnp.float32)
        output = jnp.einsum('thqk,tkhd->qhd', weights, tile_values)
        delta_rows = lax.optimization_barrier(jnp.sum(grads * output, axis=2))
        grad_probs = jnp.einsum('qhd,tkhd->thqk', grads, tile_values)
        grad_scores = probabilities * (grad_probs - delta_rows.T[None, :, :, None])
        grad_scores = lax.optimization_barrier(grad_scores.astype(jnp.bfloat16)).astype(jnp.float32)
        grad_queries = jnp.einsum('thqk,tkhd->qhd', grad_scores, tile_keys) * score_scale
        key_terms = jnp.einsum('thqk,qhd->tkhd', grad_scores, queries)
        value_terms = jnp.einsum('thqk,qhd->tkhd', weights, grads)
        sum_keys = sum_keys.at[row_list].add(key_terms)
        sum_values = sum_values.at[row_list].add(value_terms)
        return ((sum_keys, sum_values), grad_queries.astype(jnp.bfloat16))
    zeros_start = jnp.zeros((blocks, length, HEADS, head_size), jnp.float32)
    (sum_keys, sum_values), query_context = lax.scan(visit_block, (zeros_start, zeros_start), jnp.arange(blocks, dtype=jnp.int32))
    row_blocks = jnp.arange(blocks, dtype=jnp.int32)
    context_of_row = (row_blocks // N_INNER * N_INNER + layout[row_blocks % N_INNER]).astype(jnp.int32)
    grad_query = query_context[context_of_row].reshape(query_vec.shape)
    grad_key = (sum_keys * score_scale).astype(jnp.bfloat16).reshape(query_vec.shape)
    grad_value = sum_values.astype(jnp.bfloat16).reshape(query_vec.shape)
    return (grad_query, grad_key, grad_value)
```

```python
import functools
import math

import jax
import jax.numpy as jnp
from jax import lax
from jax.experimental import pallas as pl
from jax.experimental.pallas import tpu as pltpu
from jax.sharding import PartitionSpec as P

HEADS = 2
HD = 128
TOPK = 3
OWN = TOPK
TILE = 16
CHUNK = 256
MESH = pl.DeviceIdType.MESH
F32 = jnp.float32
BF16 = jnp.bfloat16
SCALE = 1.0 / math.sqrt(HD)
EXP2_SCALE = SCALE * math.log2(math.e)


def dot(a, b):
    return jnp.dot(a, b, preferred_element_type=F32)


def fold(x, op):
    return op(x.reshape(x.shape[0] // 8, 8, x.shape[1]), axis=0)


def compute_head(h, picked, q, g, kv, kt, s_scr, dp_scr, dqt, dk, dv, gq_ref):
    length = q.shape[1]
    blocks = length // CHUNK

    for t in range(TOPK + 1):
        kt[t] = kv[h, t, :length].T
    dk[h] = jnp.zeros(dk.shape[1:], F32)
    dv[h] = jnp.zeros(dv.shape[1:], F32)

    def rows(t, b, base=0):
        return kv[h, t, pl.ds(pl.multiple_of(base + b * CHUNK, CHUNK), CHUNK)]

    def chunk(j, carry):
        here = pl.ds(pl.multiple_of(j * CHUNK, CHUNK), CHUNK)
        qc, gc = q[h, here], g[h, here]
        qtc, gtc = qc.T, gc.T
        low = jnp.full((8, CHUNK), -jnp.inf, F32)

        def scores(t, b, m):
            s = dot(rows(t, b), qtc)
            s_scr[t * blocks + b] = s
            return jnp.maximum(m, fold(s, jnp.max))

        def far_max(t, m):
            mt = low
            for b in range(blocks):
                mt = scores(t, b, mt)
            return jnp.maximum(m, jnp.where(picked(t), mt, -jnp.inf))

        m = lax.fori_loop(0, TOPK, far_max, low)
        m = lax.fori_loop(0, j, lambda b, m: scores(OWN, b, m), m)
        s = dot(rows(OWN, j), qtc)
        at = lambda d: lax.broadcasted_iota(jnp.int32, (CHUNK, CHUNK), d)
        s = jnp.where(at(0) <= at(1), s, -jnp.inf)
        s_scr[OWN * blocks + j] = s
        m = jnp.maximum(m, fold(s, jnp.max))
        top = jnp.max(m, axis=0, keepdims=True) * EXP2_SCALE

        def weigh(t, b, shift, sums):
            total, mixed = sums
            e = jnp.exp2(s_scr[t * blocks + b] * EXP2_SCALE - shift)
            dp = dot(rows(t, b, length), gtc)
            s_scr[t * blocks + b] = e
            dp_scr[t * blocks + b] = dp
            return total + fold(e, jnp.sum), mixed + fold(e * dp, jnp.sum)

        def far_weigh(t, sums):
            shift = jnp.where(picked(t), top, jnp.inf)
            for b in range(blocks):
                sums = weigh(t, b, shift, sums)
            return sums

        zero = jnp.zeros((8, CHUNK), F32)
        sums = lax.fori_loop(0, TOPK, far_weigh, (zero, zero))
        sums = lax.fori_loop(0, j + 1, lambda b, s: weigh(OWN, b, top, s), sums)
        inverse = 1.0 / jnp.sum(sums[0], axis=0, keepdims=True)
        delta = jnp.sum(sums[1], axis=0, keepdims=True) * inverse

        dqt[...] = jnp.zeros(dqt.shape, F32)

        def grads(t, b):
            p = s_scr[t * blocks + b] * inverse
            ds = (p * (dp_scr[t * blocks + b] - delta)).astype(BF16)
            there = pl.ds(pl.multiple_of(b * CHUNK, CHUNK), CHUNK)
            dv[h, t, there] += dot(p.astype(BF16), gc)
            dk[h, t, there] += dot(ds, qc)
            dqt[...] += dot(kt[t, :, there], ds)

        def far_grads(t, c):
            for b in range(blocks):
                grads(t, b)
            return c

        lax.fori_loop(0, TOPK, far_grads, 0)
        lax.fori_loop(0, j + 1, lambda b, c: (grads(OWN, b), c)[1], 0)
        gq_ref[here, h * HD : (h + 1) * HD] = (dqt[...].T * SCALE).astype(BF16)
        return carry

    lax.fori_loop(0, blocks, chunk, 0)


def kernel(
    n_outer, n_inner,
    chosen, layout, q_in, k_in, v_in, g_in,
    gq_ref, gk_ref, gv_ref,
    inverse, wanted, hot_rows, hot, q, g, kv, kt, s_scr, dp_scr, dqt, dk, dv,
    relay0, relay1, outgoing, terms, landed, wide, summed, back,
    in_sem, send_sem, recv_sem,
):
    devices = n_outer * n_inner
    relay = (relay0, relay1)
    my_outer, my_inner = lax.axis_index("outer"), lax.axis_index("inner")
    me = my_outer * n_inner + my_inner
    length = q.shape[1]

    def peer(s):
        o = lax.rem(my_outer + lax.div(s, n_inner), n_outer)
        i = lax.rem(my_inner + lax.rem(s, n_inner), n_inner)
        return o * n_inner + i, (o, i)

    barrier = pltpu.get_barrier_semaphore()

    def greet(s, c):
        pl.semaphore_signal(barrier, inc=1, device_id=peer(s)[1], device_id_type=MESH)
        return c

    lax.fori_loop(1, devices, greet, 0)

    loads = []
    for h in range(HEADS):
        cols = pl.ds(h * HD, HD)
        for src, dst in (
            (k_in, kv.at[h, OWN, pl.ds(0, length)]),
            (v_in, kv.at[h, OWN, pl.ds(length, length)]),
            (q_in, q.at[h]),
            (g_in, g.at[h]),
        ):
            copy = pltpu.make_async_copy(src.at[:, cols], dst, in_sem.at[len(loads)])
            copy.start()
            loads.append(copy)

    def invert(p, c):
        inverse[p] = sum(jnp.where(layout[j] == p, j, 0) for j in range(n_inner))
        return c

    lax.fori_loop(0, n_inner, invert, 0)
    lane = lax.broadcasted_iota(jnp.int32, (1, devices), 1)

    def want(r, c):
        block = lax.div(r, n_inner) * n_inner + layout[lax.rem(r, n_inner)]
        for t in range(TOPK):
            picked = chosen[block, t]
            row = lax.div(picked, n_inner) * n_inner + inverse[lax.rem(picked, n_inner)]
            wanted[r * TOPK + t] = row
            hot_rows[pl.ds(r * TOPK + t, 1), :] = jnp.where(lane == row, 1.0, 0.0)
        return c

    lax.fori_loop(0, devices, want, 0)
    hot[...] = hot_rows[...].T.astype(BF16)
    my_block = my_outer * n_inner + layout[my_inner]

    def picked(t):
        return chosen[my_block, t] < my_block

    for copy in loads:
        copy.wait()
    pl.semaphore_wait(barrier, devices - 1)

    def exchange(phase, src_of, dst):
        send, recv = send_sem.at[phase], recv_sem.at[phase]
        pltpu.make_async_copy(src_of(me), dst, recv).start()

        def go(s, c):
            r, where = peer(s)
            pltpu.make_async_remote_copy(
                src_ref=src_of(r), dst_ref=dst, send_sem=send, recv_sem=recv,
                device_id=where, device_id_type=MESH,
            ).start()
            return c

        lax.fori_loop(1, devices, go, 0)

    def arrived(phase, whole):
        pltpu.make_async_copy(whole, whole, recv_sem.at[phase]).wait()

    def place(r):
        return pl.ds(pl.multiple_of(r * TILE, TILE), TILE)

    far = lambda h: kv.at[h, pl.ds(0, TOPK)]

    for h in range(HEADS):
        exchange(h, lambda r: kv.at[h, OWN, place(r)], relay[h].at[me])

    for h in range(HEADS):
        arrived(h, relay[h])

        def pick(r, c):
            for t in range(TOPK):
                outgoing[h, r, t] = relay[h][wanted[r * TOPK + t]]
            return c

        lax.fori_loop(0, devices, pick, 0)
        exchange(2 + h, lambda r: outgoing.at[h, r], kv.at[h, pl.ds(0, TOPK), place(me)])

    for h in range(HEADS):
        arrived(2 + h, far(h))
        compute_head(h, picked, q, g, kv, kt, s_scr, dp_scr, dqt, dk, dv, gq_ref)
        for t in range(TOPK):
            terms[h, t, :length] = dk[h, t].astype(BF16)
            terms[h, t, length:] = dv[h, t].astype(BF16)
        exchange(4 + h, lambda r: terms.at[h, :, place(r)], landed.at[h, me])

    for h in range(HEADS):
        arrived(4 + h, landed.at[h])

        def widen(r, c):
            wide[pl.ds(r * TOPK * TILE, TOPK * TILE)] = (
                landed[h, r].astype(F32).reshape(TOPK * TILE, HD)
            )
            return c

        lax.fori_loop(0, devices, widen, 0)
        sums = []
        for s in range(TILE):
            part = wide[pl.ds(s, devices * TOPK, TILE), :].astype(BF16)
            sums.append(dot(hot[...], part))
        for s in range(TILE):
            wide[pl.ds(s, devices, TILE), :] = sums[s]
        summed[h] = wide[: devices * TILE].astype(BF16)
        exchange(6 + h, lambda r: summed.at[h, place(r)], back.at[h, place(me)])

    for h in range(HEADS):
        arrived(6 + h, back.at[h])
        cols = pl.ds(h * HD, HD)
        gk_ref[:, cols] = ((dk[h, OWN] + back[h, :length].astype(F32)) * SCALE).astype(BF16)
        gv_ref[:, cols] = (dv[h, OWN] + back[h, length:].astype(F32)).astype(BF16)

    def sent(phase, part):
        pltpu.make_async_copy(part, part, send_sem.at[phase]).wait()

    for h in range(HEADS):
        sent(h, relay[h].at[pl.ds(1, devices - 1)])
        sent(2 + h, outgoing.at[h, pl.ds(1, devices - 1)])
        sent(4 + h, landed.at[h, pl.ds(1, devices - 1)])
        sent(6 + h, summed.at[h, pl.ds(TILE, (devices - 1) * TILE)])


def on_device(query_vec, key_vec, value_vec, grad_out, chosen, layout):
    n_outer, n_inner = lax.axis_size("outer"), lax.axis_size("inner")
    devices = n_outer * n_inner
    length, width = query_vec.shape
    blocks = length // CHUNK
    out = jax.ShapeDtypeStruct((length, width), BF16)
    scratch = [
        pltpu.SMEM((n_inner,), jnp.int32),
        pltpu.SMEM((devices * TOPK,), jnp.int32),
        pltpu.VMEM((devices * TOPK, devices), F32),
        pltpu.VMEM((devices, devices * TOPK), BF16),
        pltpu.VMEM((HEADS, length, HD), BF16),
        pltpu.VMEM((HEADS, length, HD), BF16),
        pltpu.VMEM((HEADS, TOPK + 1, 2 * length, HD), BF16),
        pltpu.VMEM((TOPK + 1, HD, length), BF16),
        pltpu.VMEM(((TOPK + 1) * blocks, CHUNK, CHUNK), F32),
        pltpu.VMEM(((TOPK + 1) * blocks, CHUNK, CHUNK), F32),
        pltpu.VMEM((HD, CHUNK), F32),
        pltpu.VMEM((HEADS, TOPK + 1, length, HD), F32),
        pltpu.VMEM((HEADS, TOPK + 1, length, HD), F32),
        pltpu.VMEM((devices, TILE, HD), BF16),
        pltpu.VMEM((devices, TILE, HD), BF16),
        pltpu.VMEM((HEADS, devices, TOPK, TILE, HD), BF16),
        pltpu.VMEM((HEADS, TOPK, 2 * length, HD), BF16),
        pltpu.VMEM((HEADS, devices, TOPK, TILE, HD), BF16),
        pltpu.VMEM((devices * TOPK * TILE, HD), F32),
        pltpu.VMEM((HEADS, devices * TILE, HD), BF16),
        pltpu.VMEM((HEADS, devices * TILE, HD), BF16),
        pltpu.SemaphoreType.DMA((4 * HEADS,)),
        pltpu.SemaphoreType.DMA((4 * HEADS,)),
        pltpu.SemaphoreType.DMA((4 * HEADS,)),
    ]
    return pl.pallas_call(
        functools.partial(kernel, n_outer, n_inner),
        out_shape=(out, out, out),
        in_specs=[pl.BlockSpec(memory_space=pltpu.SMEM)] * 2
        + [pl.BlockSpec(memory_space=pl.ANY)] * 4,
        out_specs=(pl.BlockSpec(memory_space=pltpu.VMEM),) * 3,
        scratch_shapes=scratch,
        compiler_params=pltpu.CompilerParams(
            collective_id=0, has_side_effects=True, vmem_limit_bytes=58 << 20
        ),
    )(chosen, layout, query_vec, key_vec, value_vec, grad_out)


def solution(mesh):
    rows = P(("outer", "inner"), None)
    return jax.shard_map(
        on_device,
        mesh=mesh,
        in_specs=(rows, rows, rows, rows, P(), P()),
        out_specs=(rows, rows, rows),
        check_vma=False,
    )
```

```python
import functools
import math

import jax
import jax.numpy as jnp
from jax import lax
from jax.experimental import pallas as pl
from jax.experimental.pallas import tpu as pltpu
from jax.sharding import PartitionSpec as P

HEADS = 2
HD = 128
TOPK = 3
OWN = TOPK
TILE = 16
KEYS = 256
MESH = pl.DeviceIdType.MESH
F32 = jnp.float32
BF16 = jnp.bfloat16
SCALE = 1.0 / math.sqrt(HD)
EXP2_SCALE = SCALE * math.log2(math.e)


def dot(a, b):
    return jnp.dot(a, b, preferred_element_type=F32)


def fold(x, op):
    return op(x.reshape(x.shape[0] // 8, 8, x.shape[1]), axis=0)


def block_rows(ref, h, t, b, base=0):
    return ref[h, t, pl.ds(pl.multiple_of(base + b * KEYS, KEYS), KEYS)]


def causal(shape):
    at = lambda d: lax.broadcasted_iota(jnp.int32, shape, d)
    return at(0) <= at(1)


def own_scores(h, b, qt, kv):
    s = dot(block_rows(kv, h, OWN, b), qt[h, :, b * KEYS :])
    return jnp.where(causal(s.shape), s * EXP2_SCALE, -jnp.inf)


def own_stats(h, qt, gt, kv, s_scr, stats, parts):
    length = qt.shape[2]
    blocks = length // KEYS
    parts[0] = jnp.full((8, length), -jnp.inf, F32)
    parts[1] = jnp.zeros((8, length), F32)
    parts[2] = jnp.zeros((8, length), F32)
    for b in range(blocks):
        s = own_scores(h, b, qt, kv)
        s_scr[b, :, b * KEYS :] = s
        parts[0, :, b * KEYS :] = jnp.maximum(parts[0, :, b * KEYS :], fold(s, jnp.max))
    stats[h, 0:1] = jnp.max(parts[0], axis=0, keepdims=True)
    for b in range(blocks):
        e = jnp.exp2(s_scr[b, :, b * KEYS :] - stats[h, 0:1, b * KEYS :])
        dp = dot(block_rows(kv, h, OWN, b, length), gt[h, :, b * KEYS :])
        parts[1, :, b * KEYS :] += fold(e, jnp.sum)
        parts[2, :, b * KEYS :] += fold(e * dp, jnp.sum)
    stats[h, 1:2] = jnp.sum(parts[1], axis=0, keepdims=True)
    stats[h, 2:3] = jnp.sum(parts[2], axis=0, keepdims=True)


def far_grads(h, picked, q, g, qt, gt, kv, kt, s_scr, dp_scr, stats, dqt, terms):
    length = q.shape[1]
    blocks = length // KEYS
    for t in range(TOPK):
        kt[t] = kv[h, t, :length].T

    def find_max(t, m):
        mt = jnp.full((8, length), -jnp.inf, F32)
        for b in range(blocks):
            s = dot(block_rows(kv, h, t, b), qt[h])
            s_scr[t * blocks + b] = s
            mt = jnp.maximum(mt, fold(s, jnp.max))
        return jnp.maximum(m, jnp.where(picked(t), mt, -jnp.inf))

    m = lax.fori_loop(0, TOPK, find_max, jnp.full((8, length), -jnp.inf, F32))
    own_top = stats[h, 0:1]
    top = jnp.maximum(jnp.max(m, axis=0, keepdims=True) * EXP2_SCALE, own_top)

    def weigh(t, sums):
        total, mixed = sums
        shift = jnp.where(picked(t), top, jnp.inf)
        for b in range(blocks):
            e = jnp.exp2(s_scr[t * blocks + b] * EXP2_SCALE - shift)
            dp = dot(block_rows(kv, h, t, b, length), gt[h])
            s_scr[t * blocks + b] = e
            dp_scr[t * blocks + b] = dp
            total, mixed = total + fold(e, jnp.sum), mixed + fold(e * dp, jnp.sum)
        return total, mixed

    zero = jnp.zeros((8, length), F32)
    total, mixed = lax.fori_loop(0, TOPK, weigh, (zero, zero))
    keep = jnp.exp2(own_top - top)
    total = jnp.sum(total, axis=0, keepdims=True) + stats[h, 1:2] * keep
    inverse = 1.0 / total
    delta = (jnp.sum(mixed, axis=0, keepdims=True) + stats[h, 2:3] * keep) * inverse
    stats[h, 3:4] = top + jnp.log2(total)
    stats[h, 4:5] = delta
    dqt[h] = jnp.zeros(dqt.shape[1:], F32)

    def grads(t, c):
        for b in range(blocks):
            p = s_scr[t * blocks + b] * inverse
            ds = (p * (dp_scr[t * blocks + b] - delta)).astype(BF16)
            rows = pl.ds(b * KEYS, KEYS)
            terms[h, t, rows] = dot(ds, q[h]).astype(BF16)
            terms[h, t, pl.ds(length + b * KEYS, KEYS)] = dot(p.astype(BF16), g[h]).astype(BF16)
            dqt[h] += dot(kt[t, :, rows], ds)
        return c

    lax.fori_loop(0, TOPK, grads, 0)


def own_grads(h, q, g, qt, gt, kv, kt, stats, dqt, dk, dv, gq_ref):
    length = q.shape[1]
    kt[OWN] = kv[h, OWN, :length].T
    for b in range(length // KEYS):
        lanes = slice(b * KEYS, length)
        p = jnp.exp2(own_scores(h, b, qt, kv) - stats[h, 3:4, lanes])
        dp = dot(block_rows(kv, h, OWN, b, length), gt[h, :, lanes])
        ds = (p * (dp - stats[h, 4:5, lanes])).astype(BF16)
        rows = slice(b * KEYS, (b + 1) * KEYS)
        dk[h, rows] = dot(ds, q[h, lanes])
        dv[h, rows] = dot(p.astype(BF16), g[h, lanes])
        dqt[h, :, lanes] += dot(kt[OWN, :, rows], ds)
    gq_ref[:, h * HD : (h + 1) * HD] = (dqt[h].T * SCALE).astype(BF16)


def kernel(
    n_outer, n_inner,
    chosen, layout, q_in, k_in, v_in, g_in,
    gq_ref, gk_ref, gv_ref,
    inverse, wanted, hot_rows, hot, q, g, qt, gt, kv, kt, s_scr, dp_scr, stats, parts, dqt, dk, dv,
    relay0, relay1, outgoing, terms, landed, wide, summed, back,
    in_sem, send_sem, recv_sem,
):
    devices = n_outer * n_inner
    relay = (relay0, relay1)
    my_outer, my_inner = lax.axis_index("outer"), lax.axis_index("inner")
    me = my_outer * n_inner + my_inner
    length = q.shape[1]

    def peer(s):
        o = lax.rem(my_outer + lax.div(s, n_inner), n_outer)
        i = lax.rem(my_inner + lax.rem(s, n_inner), n_inner)
        return o * n_inner + i, (o, i)

    loads = []
    for h in range(HEADS):
        cols = pl.ds(h * HD, HD)
        for src, dst in (
            (k_in, kv.at[h, OWN, pl.ds(0, length)]),
            (v_in, kv.at[h, OWN, pl.ds(length, length)]),
            (q_in, q.at[h]),
            (g_in, g.at[h]),
        ):
            copy = pltpu.make_async_copy(src.at[:, cols], dst, in_sem.at[len(loads)])
            copy.start()
            loads.append(copy)

    barrier = pltpu.get_barrier_semaphore()

    def greet(s, c):
        pl.semaphore_signal(barrier, inc=1, device_id=peer(s)[1], device_id_type=MESH)
        return c

    lax.fori_loop(1, devices, greet, 0)
    for copy in loads:
        copy.wait()

    def exchange(phase, src_of, dst):
        send, recv = send_sem.at[phase], recv_sem.at[phase]
        pltpu.make_async_copy(src_of(me), dst, recv).start()

        def go(s, c):
            r, where = peer(s)
            pltpu.make_async_remote_copy(
                src_ref=src_of(r), dst_ref=dst, send_sem=send, recv_sem=recv,
                device_id=where, device_id_type=MESH,
            ).start()
            return c

        lax.fori_loop(1, devices, go, 0)

    def arrived(phase, whole):
        pltpu.make_async_copy(whole, whole, recv_sem.at[phase]).wait()

    def sent(phase, part):
        pltpu.make_async_copy(part, part, send_sem.at[phase]).wait()

    def place(r):
        return pl.ds(pl.multiple_of(r * TILE, TILE), TILE)

    others = pl.ds(1, devices - 1)

    def spread(h):
        exchange(h, lambda r: kv.at[h, OWN, place(r)], relay[h].at[me])

    def serve(h):
        exchange(2 + h, lambda r: outgoing.at[h, r], kv.at[h, pl.ds(0, TOPK), place(me)])

    def pick(h):
        arrived(h, relay[h])

        def one(r, c):
            for t in range(TOPK):
                outgoing[h, r, t] = relay[h][wanted[r * TOPK + t]]
            return c

        lax.fori_loop(0, devices, one, 0)

    def work(h):
        arrived(2 + h, kv.at[h, pl.ds(0, TOPK)])
        far_grads(h, picked, q, g, qt, gt, kv, kt, s_scr, dp_scr, stats, dqt, terms)
        exchange(4 + h, lambda r: terms.at[h, :, place(r)], landed.at[h, me])

    def add_up(h):
        arrived(4 + h, landed.at[h])

        def widen(r, c):
            wide[pl.ds(r * TOPK * TILE, TOPK * TILE)] = (
                landed[h, r].astype(F32).reshape(TOPK * TILE, HD)
            )
            return c

        lax.fori_loop(0, devices, widen, 0)
        sums = []
        for s in range(TILE):
            part = wide[pl.ds(s, devices * TOPK, TILE), :].astype(BF16)
            sums.append(dot(hot[...], part))
        for s in range(TILE):
            wide[pl.ds(s, devices, TILE), :] = sums[s]
        summed[h] = wide[: devices * TILE].astype(BF16)
        exchange(6 + h, lambda r: summed.at[h, place(r)], back.at[h, place(me)])

    def finish(h):
        arrived(6 + h, back.at[h])
        cols = pl.ds(h * HD, HD)
        gk_ref[:, cols] = ((dk[h] + back[h, :length].astype(F32)) * SCALE).astype(BF16)
        gv_ref[:, cols] = (dv[h] + back[h, length:].astype(F32)).astype(BF16)

    pl.semaphore_wait(barrier, devices - 1)
    spread(0)

    def invert(p, c):
        inverse[p] = sum(jnp.where(layout[j] == p, j, 0) for j in range(n_inner))
        return c

    lax.fori_loop(0, n_inner, invert, 0)
    lane = lax.broadcasted_iota(jnp.int32, (1, devices), 1)

    def want(r, c):
        block = lax.div(r, n_inner) * n_inner + layout[lax.rem(r, n_inner)]
        for t in range(TOPK):
            row = chosen[t, block]
            row = lax.div(row, n_inner) * n_inner + inverse[lax.rem(row, n_inner)]
            wanted[r * TOPK + t] = row
            hot_rows[pl.ds(r * TOPK + t, 1), :] = jnp.where(lane == row, 1.0, 0.0)
        return c

    lax.fori_loop(0, devices, want, 0)
    my_block = my_outer * n_inner + layout[my_inner]

    def picked(t):
        return chosen[t, my_block] < my_block

    sent(0, relay[0].at[others])
    spread(1)
    hot[...] = hot_rows[...].T.astype(BF16)
    for h in range(HEADS):
        qt[h] = q[h].T
        gt[h] = g[h].T
    pick(0)
    serve(0)
    for h in range(HEADS):
        own_stats(h, qt, gt, kv, s_scr, stats, parts)
    pick(1)
    sent(2, outgoing.at[0, others])
    serve(1)
    work(0)
    work(1)
    for h in range(HEADS):
        own_grads(h, q, g, qt, gt, kv, kt, stats, dqt, dk, dv, gq_ref)
        add_up(h)
    for h in range(HEADS):
        finish(h)
    sent(1, relay[1].at[others])
    sent(3, outgoing.at[1, others])
    for h in range(HEADS):
        sent(4 + h, landed.at[h, others])
        sent(6 + h, summed.at[h, pl.ds(TILE, (devices - 1) * TILE)])


def on_device(query_vec, key_vec, value_vec, grad_out, chosen, layout):
    n_outer, n_inner = lax.axis_size("outer"), lax.axis_size("inner")
    devices = n_outer * n_inner
    length, width = query_vec.shape
    blocks = length // KEYS
    out = jax.ShapeDtypeStruct((length, width), BF16)
    scratch = [
        pltpu.SMEM((n_inner,), jnp.int32),
        pltpu.SMEM((devices * TOPK,), jnp.int32),
        pltpu.VMEM((devices * TOPK, devices), F32),
        pltpu.VMEM((devices, devices * TOPK), BF16),
        pltpu.VMEM((HEADS, length, HD), BF16),
        pltpu.VMEM((HEADS, length, HD), BF16),
        pltpu.VMEM((HEADS, HD, length), BF16),
        pltpu.VMEM((HEADS, HD, length), BF16),
        pltpu.VMEM((HEADS, TOPK + 1, 2 * length, HD), BF16),
        pltpu.VMEM((TOPK + 1, HD, length), BF16),
        pltpu.VMEM((TOPK * blocks, KEYS, length), F32),
        pltpu.VMEM((TOPK * blocks, KEYS, length), F32),
        pltpu.VMEM((HEADS, 8, length), F32),
        pltpu.VMEM((3, 8, length), F32),
        pltpu.VMEM((HEADS, HD, length), F32),
        pltpu.VMEM((HEADS, length, HD), F32),
        pltpu.VMEM((HEADS, length, HD), F32),
        pltpu.VMEM((devices, TILE, HD), BF16),
        pltpu.VMEM((devices, TILE, HD), BF16),
        pltpu.VMEM((HEADS, devices, TOPK, TILE, HD), BF16),
        pltpu.VMEM((HEADS, TOPK, 2 * length, HD), BF16),
        pltpu.VMEM((HEADS, devices, TOPK, TILE, HD), BF16),
        pltpu.VMEM((devices * TOPK * TILE, HD), F32),
        pltpu.VMEM((HEADS, devices * TILE, HD), BF16),
        pltpu.VMEM((HEADS, devices * TILE, HD), BF16),
        pltpu.SemaphoreType.DMA((4 * HEADS,)),
        pltpu.SemaphoreType.DMA((4 * HEADS,)),
        pltpu.SemaphoreType.DMA((4 * HEADS,)),
    ]
    return pl.pallas_call(
        functools.partial(kernel, n_outer, n_inner),
        out_shape=(out, out, out),
        in_specs=[pl.BlockSpec(memory_space=pltpu.SMEM)] * 2
        + [pl.BlockSpec(memory_space=pl.ANY)] * 4,
        out_specs=(pl.BlockSpec(memory_space=pltpu.VMEM),) * 3,
        scratch_shapes=scratch,
        compiler_params=pltpu.CompilerParams(
            collective_id=0, has_side_effects=True, vmem_limit_bytes=58 << 20
        ),
    )(chosen.T, layout, query_vec, key_vec, value_vec, grad_out)


def solution(mesh):
    rows = P(("outer", "inner"), None)
    return jax.shard_map(
        on_device,
        mesh=mesh,
        in_specs=(rows, rows, rows, rows, P(), P()),
        out_specs=(rows, rows, rows),
        check_vma=False,
    )
```

```python
import functools
import math

import jax
import jax.numpy as jnp
from jax import lax
from jax.experimental import pallas as pl
from jax.experimental.pallas import tpu as pltpu
from jax.sharding import PartitionSpec as P

HEADS = 2
HD = 128
TOPK = 3
OWN = TOPK
TILE = 16
KEYS = 256
PARTS = 2
MESH = pl.DeviceIdType.MESH
F32 = jnp.float32
BF16 = jnp.bfloat16
SCALE = 1.0 / math.sqrt(HD)
EXP2_SCALE = SCALE * math.log2(math.e)


def dot(a, b):
    return jnp.dot(a, b, preferred_element_type=F32)


def fold(x, op):
    return op(x.reshape(x.shape[0] // 8, 8, x.shape[1]), axis=0)


def block_rows(ref, h, t, b, base=0):
    return ref[h, t, pl.ds(pl.multiple_of(base + b * KEYS, KEYS), KEYS)]


def causal(shape):
    at = lambda d: lax.broadcasted_iota(jnp.int32, shape, d)
    return at(0) <= at(1)


def own_scores(h, b, qt, kv):
    s = dot(block_rows(kv, h, OWN, b), qt[h, :, b * KEYS :])
    return jnp.where(causal(s.shape), s * EXP2_SCALE, -jnp.inf)


def own_stats(h, qt, gt, kv, s_scr, stats, parts):
    length = qt.shape[2]
    blocks = length // KEYS
    parts[0] = jnp.full((8, length), -jnp.inf, F32)
    parts[1] = jnp.zeros((8, length), F32)
    parts[2] = jnp.zeros((8, length), F32)
    for b in range(blocks):
        s = own_scores(h, b, qt, kv)
        s_scr[b, :, b * KEYS :] = s
        parts[0, :, b * KEYS :] = jnp.maximum(parts[0, :, b * KEYS :], fold(s, jnp.max))
    stats[h, 0:1] = jnp.max(parts[0], axis=0, keepdims=True)
    for b in range(blocks):
        e = jnp.exp2(s_scr[b, :, b * KEYS :] - stats[h, 0:1, b * KEYS :])
        dp = dot(block_rows(kv, h, OWN, b, length), gt[h, :, b * KEYS :])
        parts[1, :, b * KEYS :] += fold(e, jnp.sum)
        parts[2, :, b * KEYS :] += fold(e * dp, jnp.sum)
    stats[h, 1:2] = jnp.sum(parts[1], axis=0, keepdims=True)
    stats[h, 2:3] = jnp.sum(parts[2], axis=0, keepdims=True)


def far_grads(h, picked, q, g, qt, gt, kv, kt, s_scr, dp_scr, stats, dqt, terms):
    length = q.shape[1]
    blocks = length // KEYS
    for t in range(TOPK):
        kt[t] = kv[h, t, :length].T

    def find_max(t, m):
        mt = jnp.full((8, length), -jnp.inf, F32)
        for b in range(blocks):
            s = dot(block_rows(kv, h, t, b), qt[h])
            s_scr[t * blocks + b] = s
            mt = jnp.maximum(mt, fold(s, jnp.max))
        return jnp.maximum(m, jnp.where(picked(t), mt, -jnp.inf))

    m = lax.fori_loop(0, TOPK, find_max, jnp.full((8, length), -jnp.inf, F32))
    own_top = stats[h, 0:1]
    top = jnp.maximum(jnp.max(m, axis=0, keepdims=True) * EXP2_SCALE, own_top)

    def weigh(t, sums):
        total, mixed = sums
        shift = jnp.where(picked(t), top, jnp.inf)
        for b in range(blocks):
            e = jnp.exp2(s_scr[t * blocks + b] * EXP2_SCALE - shift)
            dp = dot(block_rows(kv, h, t, b, length), gt[h])
            s_scr[t * blocks + b] = e
            dp_scr[t * blocks + b] = dp
            total, mixed = total + fold(e, jnp.sum), mixed + fold(e * dp, jnp.sum)
        return total, mixed

    zero = jnp.zeros((8, length), F32)
    total, mixed = lax.fori_loop(0, TOPK, weigh, (zero, zero))
    keep = jnp.exp2(own_top - top)
    total = jnp.sum(total, axis=0, keepdims=True) + stats[h, 1:2] * keep
    inverse = 1.0 / total
    delta = (jnp.sum(mixed, axis=0, keepdims=True) + stats[h, 2:3] * keep) * inverse
    stats[h, 3:4] = top + jnp.log2(total)
    stats[h, 4:5] = delta
    dqt[h] = jnp.zeros(dqt.shape[1:], F32)

    def grads(t, c):
        for b in range(blocks):
            p = s_scr[t * blocks + b] * inverse
            ds = (p * (dp_scr[t * blocks + b] - delta)).astype(BF16)
            rows = pl.ds(b * KEYS, KEYS)
            terms[h, t, rows] = dot(ds, q[h]).astype(BF16)
            terms[h, t, pl.ds(length + b * KEYS, KEYS)] = dot(p.astype(BF16), g[h]).astype(BF16)
            dqt[h] += dot(kt[t, :, rows], ds)
        return c

    lax.fori_loop(0, TOPK, grads, 0)


def own_grads(h, q, g, qt, gt, kv, kt, stats, dqt, dk, dv, gq_ref):
    length = q.shape[1]
    kt[OWN] = kv[h, OWN, :length].T
    for b in range(length // KEYS):
        lanes = slice(b * KEYS, length)
        p = jnp.exp2(own_scores(h, b, qt, kv) - stats[h, 3:4, lanes])
        dp = dot(block_rows(kv, h, OWN, b, length), gt[h, :, lanes])
        ds = (p * (dp - stats[h, 4:5, lanes])).astype(BF16)
        rows = slice(b * KEYS, (b + 1) * KEYS)
        dk[h, rows] = dot(ds, q[h, lanes])
        dv[h, rows] = dot(p.astype(BF16), g[h, lanes])
        dqt[h, :, lanes] += dot(kt[OWN, :, rows], ds)
    gq_ref[:, h * HD : (h + 1) * HD] = (dqt[h].T * SCALE).astype(BF16)


def kernel(
    n_outer, n_inner,
    chosen, layout, q_in, k_in, v_in, g_in,
    gq_ref, gk_ref, gv_ref,
    inverse, wanted, hot_rows, hot, q, g, qt, gt, kv, kt, s_scr, dp_scr, stats, parts, dqt, dk, dv,
    relay0, relay1, outgoing, terms, landed, wide, summed, back,
    in_sem, send_sem, recv_sem,
):
    devices = n_outer * n_inner
    relay = (relay0, relay1)
    my_outer, my_inner = lax.axis_index("outer"), lax.axis_index("inner")
    me = my_outer * n_inner + my_inner
    length = q.shape[1]

    def each_peer(act):
        def one(s, c):
            o = lax.rem(my_outer + lax.div(s, n_inner), n_outer)
            i = lax.rem(my_inner + lax.rem(s, n_inner), n_inner)
            act(o * n_inner + i, (o, i))
            return c

        lax.fori_loop(1, devices, one, 0)

    loads = []
    for h in range(HEADS):
        cols = pl.ds(h * HD, HD)
        for src, dst in (
            (k_in, kv.at[h, OWN, pl.ds(0, length)]),
            (v_in, kv.at[h, OWN, pl.ds(length, length)]),
            (q_in, q.at[h]),
            (g_in, g.at[h]),
        ):
            copy = pltpu.make_async_copy(src.at[:, cols], dst, in_sem.at[len(loads)])
            copy.start()
            loads.append(copy)

    barrier = pltpu.get_barrier_semaphore()

    each_peer(
        lambda r, where: pl.semaphore_signal(
            barrier, inc=1, device_id=where, device_id_type=MESH
        )
    )
    for copy in loads:
        copy.wait()

    def exchange(phase, src_of, dst):
        send, recv = send_sem.at[phase], recv_sem.at[phase]
        pltpu.make_async_copy(src_of(me), dst, recv).start()

        def send_one(r, where):
            pltpu.make_async_remote_copy(
                src_ref=src_of(r), dst_ref=dst, send_sem=send, recv_sem=recv,
                device_id=where, device_id_type=MESH,
            ).start()

        each_peer(send_one)

    def arrived(phase, whole):
        pltpu.make_async_copy(whole, whole, recv_sem.at[phase]).wait()

    def sent(phase, part):
        pltpu.make_async_copy(part, part, send_sem.at[phase]).wait()

    def place(r):
        return pl.ds(pl.multiple_of(r * TILE, TILE), TILE)

    others = pl.ds(1, devices - 1)

    def spread(h):
        exchange(h, lambda r: kv.at[h, OWN, place(r)], relay[h].at[me])

    def serve(h):
        exchange(2 + h, lambda r: outgoing.at[h, r], kv.at[h, pl.ds(0, TOPK), place(me)])

    def pick(h):
        arrived(h, relay[h])

        def one(r, c):
            for t in range(TOPK):
                outgoing[h, r, t] = relay[h][wanted[r * TOPK + t]]
            return c

        lax.fori_loop(0, devices, one, 0)

    def work(h):
        arrived(2 + h, kv.at[h, pl.ds(0, TOPK)])
        far_grads(h, picked, q, g, qt, gt, kv, kt, s_scr, dp_scr, stats, dqt, terms)
        exchange(4 + h, lambda r: terms.at[h, :, place(r)], landed.at[h, me])

    def add_up(h):
        arrived(4 + h, landed.at[h])

        def widen(r, c):
            wide[pl.ds(r * TOPK * TILE, TOPK * TILE)] = (
                landed[h, r].astype(F32).reshape(TOPK * TILE, HD)
            )
            return c

        lax.fori_loop(0, devices, widen, 0)
        sums = []
        for s in range(TILE):
            part = wide[pl.ds(s, devices * TOPK, TILE), :].astype(BF16)
            sums.append(dot(hot[...], part))
        for s in range(TILE):
            wide[pl.ds(s, devices, TILE), :] = sums[s]
        summed[h] = wide[: devices * TILE].astype(BF16)

    def bring_home(h):
        exchange(6 + h, lambda r: summed.at[h, place(r)], back.at[h, place(me)])

    def finish(h):
        arrived(6 + h, back.at[h])
        cols = pl.ds(h * HD, HD)
        gk_ref[:, cols] = ((dk[h] + back[h, :length].astype(F32)) * SCALE).astype(BF16)
        gv_ref[:, cols] = (dv[h] + back[h, length:].astype(F32)).astype(BF16)

    pl.semaphore_wait(barrier, devices - 1)
    spread(0)

    def invert(p, c):
        inverse[p] = sum(jnp.where(layout[j] == p, j, 0) for j in range(n_inner))
        return c

    lax.fori_loop(0, n_inner, invert, 0)
    lane = lax.broadcasted_iota(jnp.int32, (1, devices), 1)

    def want(r, c):
        block = lax.div(r, n_inner) * n_inner + layout[lax.rem(r, n_inner)]
        for t in range(TOPK):
            row = chosen[t, block]
            row = lax.div(row, n_inner) * n_inner + inverse[lax.rem(row, n_inner)]
            wanted[r * TOPK + t] = row
            hot_rows[pl.ds(r * TOPK + t, 1), :] = jnp.where(lane == row, 1.0, 0.0)
        return c

    lax.fori_loop(0, devices, want, 0)
    my_block = my_outer * n_inner + layout[my_inner]

    def picked(t):
        return chosen[t, my_block] < my_block

    spread(1)
    hot[...] = hot_rows[...].T.astype(BF16)
    for h in range(HEADS):
        qt[h] = q[h].T
        gt[h] = g[h].T
    pick(0)
    serve(0)
    for h in range(HEADS):
        own_stats(h, qt, gt, kv, s_scr, stats, parts)
    pick(1)
    sent(2, outgoing.at[0, others])
    serve(1)
    work(0)
    work(1)
    for h in range(HEADS):
        own_grads(h, q, g, qt, gt, kv, kt, stats, dqt, dk, dv, gq_ref)
    add_up(0)
    sent(5, landed.at[1, others])
    bring_home(0)
    add_up(1)
    bring_home(1)
    for h in range(HEADS):
        finish(h)
    sent(0, relay[0].at[others])
    sent(1, relay[1].at[others])
    sent(3, outgoing.at[1, others])
    sent(4, landed.at[0, others])
    for h in range(HEADS):
        sent(6 + h, summed.at[h, pl.ds(TILE, (devices - 1) * TILE)])


def hand_on(*refs):
    for source, target in zip(refs[:3], refs[3:]):
        target[...] = source[...]


def on_device(query_vec, key_vec, value_vec, grad_out, chosen, layout):
    n_outer, n_inner = lax.axis_size("outer"), lax.axis_size("inner")
    devices = n_outer * n_inner
    length, width = query_vec.shape
    blocks = length // KEYS
    out = jax.ShapeDtypeStruct((length, width), BF16)
    scratch = [
        pltpu.SMEM((n_inner,), jnp.int32),
        pltpu.SMEM((devices * TOPK,), jnp.int32),
        pltpu.VMEM((devices * TOPK, devices), F32),
        pltpu.VMEM((devices, devices * TOPK), BF16),
        pltpu.VMEM((HEADS, length, HD), BF16),
        pltpu.VMEM((HEADS, length, HD), BF16),
        pltpu.VMEM((HEADS, HD, length), BF16),
        pltpu.VMEM((HEADS, HD, length), BF16),
        pltpu.VMEM((HEADS, TOPK + 1, 2 * length, HD), BF16),
        pltpu.VMEM((TOPK + 1, HD, length), BF16),
        pltpu.VMEM((TOPK * blocks, KEYS, length), F32),
        pltpu.VMEM((TOPK * blocks, KEYS, length), F32),
        pltpu.VMEM((HEADS, 8, length), F32),
        pltpu.VMEM((3, 8, length), F32),
        pltpu.VMEM((HEADS, HD, length), F32),
        pltpu.VMEM((HEADS, length, HD), F32),
        pltpu.VMEM((HEADS, length, HD), F32),
        pltpu.VMEM((devices, TILE, HD), BF16),
        pltpu.VMEM((devices, TILE, HD), BF16),
        pltpu.VMEM((HEADS, devices, TOPK, TILE, HD), BF16),
        pltpu.VMEM((HEADS, TOPK, 2 * length, HD), BF16),
        pltpu.VMEM((HEADS, devices, TOPK, TILE, HD), BF16),
        pltpu.VMEM((devices * TOPK * TILE, HD), F32),
        pltpu.VMEM((HEADS, devices * TILE, HD), BF16),
        pltpu.VMEM((HEADS, devices * TILE, HD), BF16),
        pltpu.SemaphoreType.DMA((4 * HEADS,)),
        pltpu.SemaphoreType.DMA((4 * HEADS,)),
        pltpu.SemaphoreType.DMA((4 * HEADS,)),
    ]
    results = pl.pallas_call(
        functools.partial(kernel, n_outer, n_inner),
        out_shape=(out, out, out),
        in_specs=[pl.BlockSpec(memory_space=pltpu.SMEM)] * 2
        + [pl.BlockSpec(memory_space=pl.ANY)] * 4,
        out_specs=(pl.BlockSpec(memory_space=pltpu.VMEM),) * 3,
        scratch_shapes=scratch,
        compiler_params=pltpu.CompilerParams(
            collective_id=0, has_side_effects=True, vmem_limit_bytes=58 << 20
        ),
    )(chosen.T, layout, query_vec, key_vec, value_vec, grad_out)
    return pl.pallas_call(
        hand_on,
        out_shape=(out, out, out),
        grid=(PARTS,),
        in_specs=[pl.BlockSpec((length // PARTS, width), lambda p: (p, 0))] * 3,
        out_specs=(pl.BlockSpec((length // PARTS, width), lambda p: (p, 0)),) * 3,
    )(*results)


def solution(mesh):
    rows = P(("outer", "inner"), None)
    return jax.shard_map(
        on_device,
        mesh=mesh,
        in_specs=(rows, rows, rows, rows, P(), P()),
        out_specs=(rows, rows, rows),
        check_vma=False,
    )
```

```python
import functools
import math

import jax
import jax.numpy as jnp
from jax import lax
from jax.experimental import pallas as pl
from jax.experimental.pallas import tpu as pltpu
from jax.sharding import PartitionSpec as P

HEADS = 2
HD = 128
TOPK = 3
OWN = TOPK
TILE = 16
KEYS = 256
PARTS = 2
MESH = pl.DeviceIdType.MESH
F32 = jnp.float32
BF16 = jnp.bfloat16
SCALE = 1.0 / math.sqrt(HD)
EXP2_SCALE = SCALE * math.log2(math.e)


def dot(a, b):
    return jnp.dot(a, b, preferred_element_type=F32)


def fold(x, op):
    return op(x.reshape(x.shape[0] // 8, 8, x.shape[1]), axis=0)


def block_rows(ref, h, t, b, base=0):
    return ref[h, t, pl.ds(pl.multiple_of(base + b * KEYS, KEYS), KEYS)]


def causal(shape):
    at = lambda d: lax.broadcasted_iota(jnp.int32, shape, d)
    return at(0) <= at(1)


def own_scores(h, b, qt, kv):
    s = dot(block_rows(kv, h, OWN, b), qt[h, :, b * KEYS :])
    return jnp.where(causal(s.shape), s * EXP2_SCALE, -jnp.inf)


def own_stats(h, qt, gt, kv, s_scr, stats, parts):
    length = qt.shape[2]
    blocks = length // KEYS
    parts[0] = jnp.full((8, length), -jnp.inf, F32)
    parts[1] = jnp.zeros((8, length), F32)
    parts[2] = jnp.zeros((8, length), F32)
    for b in range(blocks):
        s = own_scores(h, b, qt, kv)
        s_scr[b, :, b * KEYS :] = s
        parts[0, :, b * KEYS :] = jnp.maximum(parts[0, :, b * KEYS :], fold(s, jnp.max))
    stats[h, 0:1] = jnp.max(parts[0], axis=0, keepdims=True)
    for b in range(blocks):
        e = jnp.exp2(s_scr[b, :, b * KEYS :] - stats[h, 0:1, b * KEYS :])
        dp = dot(block_rows(kv, h, OWN, b, length), gt[h, :, b * KEYS :])
        parts[1, :, b * KEYS :] += fold(e, jnp.sum)
        parts[2, :, b * KEYS :] += fold(e * dp, jnp.sum)
    stats[h, 1:2] = jnp.sum(parts[1], axis=0, keepdims=True)
    stats[h, 2:3] = jnp.sum(parts[2], axis=0, keepdims=True)


def far_grads(h, picked, q, g, qt, gt, kv, kt, s_scr, dp_scr, stats, dqt, terms):
    length = q.shape[1]
    blocks = length // KEYS
    for t in range(TOPK):
        kt[t] = kv[h, t, :length].T

    def find_max(t, m):
        mt = jnp.full((8, length), -jnp.inf, F32)
        for b in range(blocks):
            s = dot(block_rows(kv, h, t, b), qt[h])
            s_scr[t * blocks + b] = s
            mt = jnp.maximum(mt, fold(s, jnp.max))
        return jnp.maximum(m, jnp.where(picked(t), mt, -jnp.inf))

    m = lax.fori_loop(0, TOPK, find_max, jnp.full((8, length), -jnp.inf, F32))
    own_top = stats[h, 0:1]
    top = jnp.maximum(jnp.max(m, axis=0, keepdims=True) * EXP2_SCALE, own_top)

    def weigh(t, sums):
        total, mixed = sums
        shift = jnp.where(picked(t), top, jnp.inf)
        for b in range(blocks):
            e = jnp.exp2(s_scr[t * blocks + b] * EXP2_SCALE - shift)
            dp = dot(block_rows(kv, h, t, b, length), gt[h])
            s_scr[t * blocks + b] = e
            dp_scr[t * blocks + b] = dp
            total, mixed = total + fold(e, jnp.sum), mixed + fold(e * dp, jnp.sum)
        return total, mixed

    zero = jnp.zeros((8, length), F32)
    total, mixed = lax.fori_loop(0, TOPK, weigh, (zero, zero))
    keep = jnp.exp2(own_top - top)
    total = jnp.sum(total, axis=0, keepdims=True) + stats[h, 1:2] * keep
    inverse = 1.0 / total
    delta = (jnp.sum(mixed, axis=0, keepdims=True) + stats[h, 2:3] * keep) * inverse
    stats[h, 3:4] = top + jnp.log2(total)
    stats[h, 4:5] = delta
    dqt[h] = jnp.zeros(dqt.shape[1:], F32)

    def grads(t, c):
        for b in range(blocks):
            p = s_scr[t * blocks + b] * inverse
            ds = (p * (dp_scr[t * blocks + b] - delta)).astype(BF16)
            rows = pl.ds(b * KEYS, KEYS)
            terms[h, t, rows] = dot(ds, q[h]).astype(BF16)
            terms[h, t, pl.ds(length + b * KEYS, KEYS)] = dot(p.astype(BF16), g[h]).astype(BF16)
            dqt[h] += dot(kt[t, :, rows], ds)
        return c

    lax.fori_loop(0, TOPK, grads, 0)


def own_grads(h, q, g, qt, gt, kv, kt, stats, dqt, dk, dv, gq_ref):
    length = q.shape[1]
    kt[OWN] = kv[h, OWN, :length].T
    for b in range(length // KEYS):
        lanes = slice(b * KEYS, length)
        p = jnp.exp2(own_scores(h, b, qt, kv) - stats[h, 3:4, lanes])
        dp = dot(block_rows(kv, h, OWN, b, length), gt[h, :, lanes])
        ds = (p * (dp - stats[h, 4:5, lanes])).astype(BF16)
        rows = slice(b * KEYS, (b + 1) * KEYS)
        dk[h, rows] = dot(ds, q[h, lanes])
        dv[h, rows] = dot(p.astype(BF16), g[h, lanes])
        dqt[h, :, lanes] += dot(kt[OWN, :, rows], ds)
    gq_ref[:, h * HD : (h + 1) * HD] = (dqt[h].T * SCALE).astype(BF16)


def kernel(
    n_outer, n_inner,
    chosen, layout, q_in, k_in, v_in, g_in,
    gq_ref, gk_ref, gv_ref,
    inverse, wanted, hot_rows, hot, q, g, qt, gt, kv, kt, s_scr, dp_scr, stats, parts, dqt, dk, dv,
    relay0, relay1, outgoing, terms, landed, wide, summed, back,
    in_sem, send_sem, recv_sem,
):
    devices = n_outer * n_inner
    relay = (relay0, relay1)
    my_outer, my_inner = lax.axis_index("outer"), lax.axis_index("inner")
    me = my_outer * n_inner + my_inner
    length = q.shape[1]

    def each_peer(act, start=1):
        def one(s, c):
            o = lax.rem(my_outer + lax.div(s, n_inner), n_outer)
            i = lax.rem(my_inner + lax.rem(s, n_inner), n_inner)
            act(o * n_inner + i, (o, i))
            return c

        lax.fori_loop(start, devices, one, 0)
        if start > 1:
            lax.fori_loop(1, start, one, 0)

    loads = []
    for h in range(HEADS):
        cols = pl.ds(h * HD, HD)
        for src, dst in (
            (k_in, kv.at[h, OWN, pl.ds(0, length)]),
            (v_in, kv.at[h, OWN, pl.ds(length, length)]),
            (q_in, q.at[h]),
            (g_in, g.at[h]),
        ):
            copy = pltpu.make_async_copy(src.at[:, cols], dst, in_sem.at[len(loads)])
            copy.start()
            loads.append(copy)

    barrier = pltpu.get_barrier_semaphore()

    each_peer(
        lambda r, where: pl.semaphore_signal(
            barrier, inc=1, device_id=where, device_id_type=MESH
        )
    )
    for copy in loads:
        copy.wait()

    def exchange(phase, src_of, dst):
        send, recv = send_sem.at[phase], recv_sem.at[phase]
        pltpu.make_async_copy(src_of(me), dst, recv).start()

        def send_one(r, where):
            pltpu.make_async_remote_copy(
                src_ref=src_of(r), dst_ref=dst, send_sem=send, recv_sem=recv,
                device_id=where, device_id_type=MESH,
            ).start()

        each_peer(send_one, 2 * n_inner if phase >= 6 else 1)

    def arrived(phase, whole):
        pltpu.make_async_copy(whole, whole, recv_sem.at[phase]).wait()

    def sent(phase, part):
        pltpu.make_async_copy(part, part, send_sem.at[phase]).wait()

    def place(r):
        return pl.ds(pl.multiple_of(r * TILE, TILE), TILE)

    others = pl.ds(1, devices - 1)

    def spread(h):
        exchange(h, lambda r: kv.at[h, OWN, place(r)], relay[h].at[me])

    def serve(h):
        exchange(2 + h, lambda r: outgoing.at[h, r], kv.at[h, pl.ds(0, TOPK), place(me)])

    def pick(h):
        arrived(h, relay[h])

        def one(r, c):
            for t in range(TOPK):
                outgoing[h, r, t] = relay[h][wanted[r * TOPK + t]]
            return c

        lax.fori_loop(0, devices, one, 0)

    def work(h):
        arrived(2 + h, kv.at[h, pl.ds(0, TOPK)])
        far_grads(h, picked, q, g, qt, gt, kv, kt, s_scr, dp_scr, stats, dqt, terms)
        exchange(4 + h, lambda r: terms.at[h, :, place(r)], landed.at[h, me])

    def add_up(h):
        arrived(4 + h, landed.at[h])

        def widen(r, c):
            wide[pl.ds(r * TOPK * TILE, TOPK * TILE)] = (
                landed[h, r].astype(F32).reshape(TOPK * TILE, HD)
            )
            return c

        lax.fori_loop(0, devices, widen, 0)
        sums = []
        for s in range(TILE):
            part = wide[pl.ds(s, devices * TOPK, TILE), :].astype(BF16)
            sums.append(dot(hot[...], part))
        for s in range(TILE):
            wide[pl.ds(s, devices, TILE), :] = sums[s]
        summed[h] = wide[: devices * TILE].astype(BF16)

    def bring_home(h):
        exchange(6 + h, lambda r: summed.at[h, place(r)], back.at[h, place(me)])

    def finish(h):
        arrived(6 + h, back.at[h])
        cols = pl.ds(h * HD, HD)
        gk_ref[:, cols] = ((dk[h] + back[h, :length].astype(F32)) * SCALE).astype(BF16)
        gv_ref[:, cols] = (dv[h] + back[h, length:].astype(F32)).astype(BF16)

    pl.semaphore_wait(barrier, devices - 1)
    spread(0)

    def invert(p, c):
        inverse[p] = sum(jnp.where(layout[j] == p, j, 0) for j in range(n_inner))
        return c

    lax.fori_loop(0, n_inner, invert, 0)
    lane = lax.broadcasted_iota(jnp.int32, (1, devices), 1)

    def want(r, c):
        block = lax.div(r, n_inner) * n_inner + layout[lax.rem(r, n_inner)]
        for t in range(TOPK):
            row = chosen[t, block]
            row = lax.div(row, n_inner) * n_inner + inverse[lax.rem(row, n_inner)]
            wanted[r * TOPK + t] = row
            hot_rows[pl.ds(r * TOPK + t, 1), :] = jnp.where(lane == row, 1.0, 0.0)
        return c

    lax.fori_loop(0, devices, want, 0)
    my_block = my_outer * n_inner + layout[my_inner]

    def picked(t):
        return chosen[t, my_block] < my_block

    spread(1)
    hot[...] = hot_rows[...].T.astype(BF16)
    for h in range(HEADS):
        qt[h] = q[h].T
        gt[h] = g[h].T
    pick(0)
    serve(0)
    for h in range(HEADS):
        own_stats(h, qt, gt, kv, s_scr, stats, parts)
    pick(1)
    sent(2, outgoing.at[0, others])
    serve(1)
    work(0)
    work(1)
    for h in range(HEADS):
        own_grads(h, q, g, qt, gt, kv, kt, stats, dqt, dk, dv, gq_ref)
    add_up(0)
    sent(5, landed.at[1, others])
    bring_home(0)
    add_up(1)
    bring_home(1)
    for h in range(HEADS):
        finish(h)
    sent(0, relay[0].at[others])
    sent(1, relay[1].at[others])
    sent(3, outgoing.at[1, others])
    sent(4, landed.at[0, others])
    for h in range(HEADS):
        sent(6 + h, summed.at[h, pl.ds(TILE, (devices - 1) * TILE)])


def hand_on(*refs):
    for source, target in zip(refs[:3], refs[3:]):
        target[...] = source[...]


def on_device(query_vec, key_vec, value_vec, grad_out, chosen, layout):
    n_outer, n_inner = lax.axis_size("outer"), lax.axis_size("inner")
    devices = n_outer * n_inner
    length, width = query_vec.shape
    blocks = length // KEYS
    out = jax.ShapeDtypeStruct((length, width), BF16)
    scratch = [
        pltpu.SMEM((n_inner,), jnp.int32),
        pltpu.SMEM((devices * TOPK,), jnp.int32),
        pltpu.VMEM((devices * TOPK, devices), F32),
        pltpu.VMEM((devices, devices * TOPK), BF16),
        pltpu.VMEM((HEADS, length, HD), BF16),
        pltpu.VMEM((HEADS, length, HD), BF16),
        pltpu.VMEM((HEADS, HD, length), BF16),
        pltpu.VMEM((HEADS, HD, length), BF16),
        pltpu.VMEM((HEADS, TOPK + 1, 2 * length, HD), BF16),
        pltpu.VMEM((TOPK + 1, HD, length), BF16),
        pltpu.VMEM((TOPK * blocks, KEYS, length), F32),
        pltpu.VMEM((TOPK * blocks, KEYS, length), F32),
        pltpu.VMEM((HEADS, 8, length), F32),
        pltpu.VMEM((3, 8, length), F32),
        pltpu.VMEM((HEADS, HD, length), F32),
        pltpu.VMEM((HEADS, length, HD), F32),
        pltpu.VMEM((HEADS, length, HD), F32),
        pltpu.VMEM((devices, TILE, HD), BF16),
        pltpu.VMEM((devices, TILE, HD), BF16),
        pltpu.VMEM((HEADS, devices, TOPK, TILE, HD), BF16),
        pltpu.VMEM((HEADS, TOPK, 2 * length, HD), BF16),
        pltpu.VMEM((HEADS, devices, TOPK, TILE, HD), BF16),
        pltpu.VMEM((devices * TOPK * TILE, HD), F32),
        pltpu.VMEM((HEADS, devices * TILE, HD), BF16),
        pltpu.VMEM((HEADS, devices * TILE, HD), BF16),
        pltpu.SemaphoreType.DMA((4 * HEADS,)),
        pltpu.SemaphoreType.DMA((4 * HEADS,)),
        pltpu.SemaphoreType.DMA((4 * HEADS,)),
    ]
    results = pl.pallas_call(
        functools.partial(kernel, n_outer, n_inner),
        out_shape=(out, out, out),
        in_specs=[pl.BlockSpec(memory_space=pltpu.SMEM)] * 2
        + [pl.BlockSpec(memory_space=pl.ANY)] * 4,
        out_specs=(pl.BlockSpec(memory_space=pltpu.VMEM),) * 3,
        scratch_shapes=scratch,
        compiler_params=pltpu.CompilerParams(
            collective_id=0, has_side_effects=True, vmem_limit_bytes=58 << 20
        ),
    )(chosen.T, layout, query_vec, key_vec, value_vec, grad_out)
    return pl.pallas_call(
        hand_on,
        out_shape=(out, out, out),
        grid=(PARTS,),
        in_specs=[pl.BlockSpec((length // PARTS, width), lambda p: (p, 0))] * 3,
        out_specs=(pl.BlockSpec((length // PARTS, width), lambda p: (p, 0)),) * 3,
    )(*results)


def solution(mesh):
    rows = P(("outer", "inner"), None)
    return jax.shard_map(
        on_device,
        mesh=mesh,
        in_specs=(rows, rows, rows, rows, P(), P()),
        out_specs=(rows, rows, rows),
        check_vma=False,
    )
```
